32 devices in a mesh: ctx: 8 (over y, x, core), dp: 4 (over z).
Axes of the slice: x: 2, y: 2, z: 4, core: 2. Of those that a mesh axis runs over, the one named last changes fastest.
Arguments:
- queries: bfloat16 [4, 1024, 16, 128], P('dp', 'ctx'), may hold values from -24 to 24
- keys: bfloat16 [4, 1024, 16, 128], P('dp', 'ctx'), may hold values from -50 to 50
- values: bfloat16 [4, 1024, 16, 128], P('dp', 'ctx'), may hold values from -6 to 6
- grad_out: bfloat16 [4, 1024, 16, 128], P('dp', 'ctx'), may hold values from -6 to 6
- memory: bfloat16 [2048, 16, 256], P(('ctx', 'dp')), may hold values from -6 to 6
- mem_index: int32 [4, 16, 16, 32], P('dp', 'ctx'), may hold values from 0 to 2047, as said below
Outputs:
- grad_queries: bfloat16 [4, 1024, 16, 128], P('dp', 'ctx')
- grad_keys: bfloat16 [4, 1024, 16, 128], P('dp', 'ctx')
- grad_values: bfloat16 [4, 1024, 16, 128], P('dp', 'ctx')
- grad_memory: bfloat16 [2048, 16, 256], P(('ctx', 'dp'))
The draws below stay inside these ranges and needn't reach their ends.
Inputs may be any that keep to these rules, and one draw needn't show every extreme that they name: `mem_index`: the rows named by one device's query blocks (all heads and retrieved rows together) lie at most 64 in any one shard of 64 consecutive memory rows, and in every draw one shard receives exactly 64 of them from every device. Rows may repeat.
All inputs are finite; a program needn't handle non-finite values.
Results may differ from the reference program's by a relative error of at most 0.015.
Values may be sent and summed in bfloat16 or wider, within the bound.
A program may use at most 128 MiB of HBM per device.

```python
import jax
import jax.numpy as jnp
from jax import lax

DH = 128
H = 16
TOPK = 32
QB = 64
MEM_DEV = 64
H_MEM = 16
SEQS = 4
CYCLE = 8
SEQ_LEN = 1024
CONTEXT = 512
BLOCKS = 16
MEM_ROWS = 2048
REQUESTS = 1024
CAP = 64


def common_parts(key):
    shape = (SEQS, SEQ_LEN, H, DH)
    shared = jax.random.truncated_normal(jax.random.fold_in(key, 101), -4.0, 4.0, shape, jnp.float32)
    return shared


def draw_queries(key, part):
    shared = common_parts(key)
    key = jax.random.fold_in(key, 1)
    return jax.random.truncated_normal(key, -4.0, 4.0, shared.shape, jnp.float32).astype(jnp.bfloat16)


def draw_keys(key, part):
    shared = common_parts(key)
    key = jax.random.fold_in(key, 2)
    return jax.random.truncated_normal(key, -4.0, 4.0, shared.shape, jnp.float32).astype(jnp.bfloat16)


def draw_mem_index(key, part):
    key = jax.random.fold_in(key, 3)
    shards = SEQS * CYCLE
    spread = jax.random.permutation(jax.random.fold_in(key, 1), shards).astype(jnp.int32)

    def one_device(number):
        sub = jax.random.fold_in(key, number + 7)
        rest = jax.random.permutation(jax.random.fold_in(sub, 1), shards * CAP - CAP)[:REQUESTS - CAP].astype(jnp.int32) + CAP
        taken = jnp.concatenate([jnp.arange(CAP, dtype=jnp.int32), rest])
        owner = spread[taken // CAP]
        local = jax.random.randint(jax.random.fold_in(sub, 2), (REQUESTS,), 0, MEM_DEV, jnp.int32)
        rows = owner * MEM_DEV + local
        return rows[jax.random.permutation(jax.random.fold_in(sub, 3), REQUESTS)]
    table = jax.vmap(one_device)(jnp.arange(shards, dtype=jnp.int32))
    return table.reshape(SEQS, BLOCKS, H_MEM, TOPK)


def block_levels(rng, shape, cuts, low, largest):
    gain, own = 1.0, jax.random.fold_in(rng, 6)
    for dim, shards_of in cuts:
        draws = jnp.exp(jax.random.uniform(jax.random.fold_in(own, dim), (shards_of,), jnp.float32, low / len(cuts), largest / len(cuts)))
        gain = gain * jnp.repeat(draws, shape[dim] // shards_of).reshape([-1 if axis == dim else 1 for axis in range(len(shape))])
    return gain


def centred(own_key, shape, deviation, limit, cuts=(), held_as=jnp.bfloat16):
    values = deviation * jax.random.normal(own_key, shape, jnp.float32)
    if cuts:
        values = values * block_levels(own_key, shape, cuts, -0.22, 0.18)
    return jnp.clip(values, -limit, limit).astype(held_as)


def setup_inputs(seed: int = 0) -> dict:
    arg_keys = jax.random.split(jax.random.key(seed), 7)
    return {
        "queries": draw_queries(jax.random.fold_in(arg_keys[6], 71), 0),
        "keys": draw_keys(jax.random.fold_in(arg_keys[6], 71), 0),
        "values": centred(arg_keys[2], (SEQS, SEQ_LEN, H, DH), 1.0, 6.0, ((0, 4), (1, 8))),
        "grad_out": centred(arg_keys[3], (SEQS, SEQ_LEN, H, DH), 1.0, 6.0, ((0, 4), (1, 8))),
        "memory": centred(arg_keys[4], (MEM_ROWS, H, 2 * DH), 1.0, 6.0, ((0, 32),)),
        "mem_index": draw_mem_index(jax.random.fold_in(arg_keys[6], 71), 0),
    }


def widen(array):
    return array.astype(jnp.float32)


def window_grads(queries, keys, values, grad_out, fetched):
    width = queries.shape[-1]
    scale = width ** -0.5
    count = queries.shape[0]
    mem_heads = fetched.shape[1]
    nblk = fetched.shape[0]
    block = count // nblk
    mem_keys = fetched[..., :width]
    mem_values = fetched[..., width:]
    scores = jnp.einsum("thd,shd->hts", widen(queries), widen(keys)) * scale
    serial = jnp.arange(count, dtype=jnp.int32)
    causal = serial[None, :] <= serial[:, None]
    scores = jnp.where(causal[None], scores, -jnp.inf)
    mem_query = queries[:, :mem_heads].reshape(nblk, block, mem_heads, width)
    mem_scores = jnp.einsum("bqhd,bhjd->hbqj", widen(mem_query), widen(mem_keys)) * scale
    top = scores.max(axis=-1)
    mem_top = jnp.maximum(top[:mem_heads], mem_scores.max(axis=-1).reshape(mem_heads, count))
    top = jnp.concatenate([mem_top, top[mem_heads:]], axis=0)
    weights = jnp.exp(scores - top[..., None])
    mem_weights = jnp.exp(mem_scores - mem_top.reshape(mem_heads, nblk, block)[..., None])
    total = weights.sum(axis=-1)
    total = jnp.concatenate([total[:mem_heads] + mem_weights.sum(axis=-1).reshape(mem_heads, count), total[mem_heads:]], axis=0)
    probs = weights / total[..., None]
    mem_probs = mem_weights / total[:mem_heads].reshape(mem_heads, nblk, block)[..., None]
    probs_low = probs.astype(jnp.bfloat16)
    mem_low = mem_probs.astype(jnp.bfloat16)
    attended = jnp.einsum("hts,shd->thd", widen(probs_low), widen(values))
    mem_attended = jnp.einsum("hbqj,bhjd->bqhd", widen(mem_low), widen(mem_values)).reshape(count, mem_heads, width)
    attended = jnp.concatenate([attended[:, :mem_heads] + mem_attended, attended[:, mem_heads:]], axis=1)
    delta = jnp.einsum("thd,thd->ht", widen(grad_out), attended)
    dprob = jnp.einsum("thd,shd->hts", widen(grad_out), widen(values))
    dscore = (probs * (dprob - delta[..., None])).astype(jnp.bfloat16)
    mem_upstream = grad_out[:, :mem_heads].reshape(nblk, block, mem_heads, width)
    mem_dprob = jnp.einsum("bqhd,bhjd->hbqj", widen(mem_upstream), widen(mem_values))
    mem_dscore = (mem_probs * (mem_dprob - delta[:mem_heads].reshape(mem_heads, nblk, block)[..., None])).astype(jnp.bfloat16)
    grad_q = jnp.einsum("hts,shd->thd", widen(dscore), widen(keys))
    mem_grad_q = jnp.einsum("hbqj,bhjd->bqhd", widen(mem_dscore), widen(mem_keys)).reshape(count, mem_heads, width)
    grad_q = jnp.concatenate([grad_q[:, :mem_heads] + mem_grad_q, grad_q[:, mem_heads:]], axis=1) * scale
    grad_k = jnp.einsum("hts,thd->shd", widen(dscore), widen(queries)) * scale
    grad_v = jnp.einsum("hts,thd->shd", widen(probs_low), widen(grad_out))
    mem_dkey = jnp.einsum("hbqj,bqhd->bhjd", widen(mem_dscore), widen(mem_query)) * scale
    mem_dvalue = jnp.einsum("hbqj,bqhd->bhjd", widen(mem_low), widen(mem_upstream))
    row_grads = jnp.concatenate([mem_dkey, mem_dvalue], axis=-1)
    return grad_q.astype(jnp.bfloat16), grad_k.astype(jnp.bfloat16), grad_v.astype(jnp.bfloat16), row_grads


def reference(queries, keys, values, grad_out, memory, mem_index):
    windows = SEQS * SEQ_LEN // CONTEXT

    def split(array):
        return array.reshape((windows, CONTEXT) + array.shape[2:])

    picks = mem_index.reshape(windows, CONTEXT // QB, H_MEM, TOPK)
    head_ids = jnp.arange(H_MEM, dtype=jnp.int32)[None, :, None]

    def one_window(operands):
        query, key_rows, value_rows, upstream, rows = operands
        fetched = memory[rows, head_ids]
        return window_grads(query, key_rows, value_rows, upstream, fetched)

    grad_q, grad_k, grad_v, row_grads = lax.map(one_window, (split(queries), split(keys), split(values), split(grad_out), picks))
    codes = (picks * H_MEM + head_ids).astype(jnp.int32).reshape(-1)
    table = jnp.zeros((MEM_ROWS * H_MEM, 2 * DH), jnp.float32).at[codes].add(row_grads.reshape(-1, 2 * DH))
    return (grad_q.reshape(queries.shape), grad_k.reshape(queries.shape), grad_v.reshape(queries.shape),
            table.reshape(MEM_ROWS, H_MEM, 2 * DH).astype(jnp.bfloat16))
```

```python
import functools

import jax
import jax.numpy as jnp
from jax import lax
from jax.experimental import pallas as pl
from jax.experimental.pallas import tpu as pltpu
from jax.sharding import PartitionSpec as P

WIN = 4
BF = jnp.bfloat16
F32 = jnp.float32
NT = (((1,), (1,)), ((), ()))
TN = (((0,), (0,)), ((), ()))


def dot(a, b, dims=(((1,), (0,)), ((), ()))):
    return lax.dot_general(a, b, dims, preferred_element_type=F32)


def kernel(
    dims,
    codes_out, table, q_ref, do_ref, kv_ref, place_col, place_row,
    dq_out, dkv_out, gin_out, codes_out2,
    codes_in, rows_out, returned, fetched, kvb, pb, rg, gout, gin,
    rb_direct, rb_cross, rb_relay, sumb,
    code_s, code_r, row_s, row_r, grad_s, grad_r,
    kv_s, kv_r, dd_s, dd_r, dc_s, dc_r, dr_s, dr_r,
):
    cycle, groups, slots, heads, width, blocks_here, topk = dims
    n = cycle * groups
    tokens = q_ref.shape[0]
    half = heads // 2
    hw = half * width
    lanes = codes_out.shape[-1]
    requests = place_row.shape[1]
    total_slots = n * slots
    scale = width ** (-0.5)
    c = lax.axis_index("ctx")
    d = lax.axis_index("dp")
    me = c * groups + d
    p = lax.rem(c, WIN)
    base = c - p
    core = lax.rem(p, 2)

    def peer_of(i):
        j = lax.rem(me + i, n)
        return j, {"ctx": j // groups, "dp": lax.rem(j, groups)}

    def pos(k):
        return {"ctx": base + k, "dp": d}

    def rcopy(src, dst, ss, rs, dev):
        return pltpu.make_async_remote_copy(
            src_ref=src, dst_ref=dst, send_sem=ss, recv_sem=rs,
            device_id=dev, device_id_type=pl.DeviceIdType.MESH,
        )

    barrier = pltpu.get_barrier_semaphore()

    def greet(i, _):
        _, dev = peer_of(i)
        pl.semaphore_signal(barrier, inc=1, device_id=dev, device_id_type=pl.DeviceIdType.MESH)
        return 0

    lax.fori_loop(1, n, greet, 0)
    pl.semaphore_wait(barrier, n - 1)

    def send_code(i, _):
        j, dev = peer_of(i)
        rcopy(codes_out.at[j], codes_in.at[me], code_s, code_r, dev).start()
        return 0

    lax.fori_loop(1, n, send_code, 0)

    def kv_send(hf, slot, target):
        return rcopy(kv_ref.at[hf], kvb.at[p, hf], kv_s.at[slot], kv_r.at[p, hf], pos(target))

    def kv_relay(b, slot):
        return rcopy(
            kvb.at[b, core], kvb.at[b, core], kv_s.at[slot], kv_r.at[b, core], pos(5 - p)
        )

    def kv_wait(b, hf):
        rcopy(kvb.at[b, hf], kvb.at[b, hf], kv_s.at[0], kv_r.at[b, hf], pos(0)).wait_recv()

    @pl.when(p < 2)
    def _():
        for hf in range(2):
            kv_send(hf, hf, 2 + hf).start()

    @pl.when(core == 0)
    def _():
        for hf in range(2):
            kv_send(hf, 2 + hf, p + 1).start()

    codes_in[me] = codes_out[me]
    kvb[p] = kv_ref[...]
    for s in range(1, WIN):
        @pl.when(s > p)
        def _():
            kvb[s] = jnp.zeros(kvb.shape[1:], BF)

    rcopy(
        codes_in.at[pl.ds(0, n - 1)], codes_in.at[pl.ds(0, n - 1)], code_s, code_r, pos(0)
    ).wait_recv()
    table_rows = table.shape[0]

    def rows_at(ref, j):
        return ref.at[pl.ds(pl.multiple_of(j * slots, slots), slots)]

    def gather(j):
        hot = lax.broadcasted_iota(jnp.int32, (table_rows, lanes), 0) == codes_in[j]
        return dot(hot.astype(F32).astype(BF), table[...], TN)[:slots].astype(BF)

    def serve(i, _):
        j, dev = peer_of(i)
        rows_out[pl.ds(pl.multiple_of(j * slots, slots), slots), :] = gather(j)
        rcopy(rows_at(rows_out, j), rows_at(returned, me), row_s, row_r, dev).start()
        return 0

    lax.fori_loop(1, n, serve, 0)
    returned[pl.ds(pl.multiple_of(me * slots, slots), slots), :] = gather(me)
    codes_out2[...] = codes_in[...]

    @pl.when(p >= 2)
    def _():
        for b in range(2):
            kv_wait(b, core)
            kv_relay(b, b).start()

    @pl.when(core == 1)
    def _():
        for hf in range(2):
            kv_wait(p - 1, hf)

    @pl.when(p >= 2)
    def _():
        for b in range(2):
            kv_wait(b, 1 - core)

    everything_else = pl.ds(0, (n - 1) * slots)

    def wait_bulk(buf, ss, rs):
        return rcopy(buf.at[everything_else], buf.at[everything_else], ss, rs, pos(0))

    wait_bulk(returned, row_s, row_r).wait_recv()

    chunk = min(128, requests)

    def pick(i, _):
        rows = pl.ds(pl.multiple_of(i * chunk, chunk), chunk)
        hot = lax.broadcasted_iota(jnp.int32, (chunk, total_slots), 1) == place_col[rows, :]
        fetched[rows, :] = dot(hot.astype(F32).astype(BF), returned[...]).astype(BF)
        return 0

    lax.fori_loop(0, requests // chunk, pick, 0)

    ctx = WIN * tokens
    per_head = blocks_here * topk
    block = tokens // blocks_here
    row_id = lax.broadcasted_iota(jnp.int32, (tokens, ctx), 0)
    col_id = lax.broadcasted_iota(jnp.int32, (tokens, ctx), 1)
    live = col_id <= row_id + p * tokens
    mrow = lax.broadcasted_iota(jnp.int32, (tokens, per_head), 0)
    mcol = lax.broadcasted_iota(jnp.int32, (tokens, per_head), 1)
    mlive = (mrow // block) == (mcol // topk)

    def head_step(hf):
        def run(hh, _):
            h = hf * half + hh
            at = pl.ds(pl.multiple_of(hh * width, width), width)
            vt = pl.ds(pl.multiple_of(hw + hh * width, width), width)
            full = pl.ds(pl.multiple_of(h * width, width), width)
            mr = pl.ds(pl.multiple_of(h * per_head, per_head), per_head)
            q = q_ref[:, full]
            do = do_ref[:, full]
            k = kvb[:, hf, :, at].reshape(ctx, width)
            v = kvb[:, hf, :, vt].reshape(ctx, width)
            mk = fetched[mr, :width]
            mv = fetched[mr, width:]
            s = jnp.where(live, dot(q, k, NT) * scale, -1e30)
            ms = jnp.where(mlive, dot(q, mk, NT) * scale, -1e30)
            top = jnp.maximum(
                jnp.max(s, axis=-1, keepdims=True), jnp.max(ms, axis=-1, keepdims=True)
            )
            w = jnp.exp(s - top)
            mw = jnp.exp(ms - top)
            inv = 1.0 / (
                jnp.sum(w, axis=-1, keepdims=True) + jnp.sum(mw, axis=-1, keepdims=True)
            )
            prob = w * inv
            mprob = mw * inv
            low = prob.astype(BF)
            mlow = mprob.astype(BF)
            dp = dot(do, v, NT)
            mdp = dot(do, mv, NT)
            delta = jnp.sum(low.astype(F32) * dp, axis=-1, keepdims=True) + jnp.sum(
                mlow.astype(F32) * mdp, axis=-1, keepdims=True
            )
            ds = (prob * (dp - delta)).astype(BF)
            mds = (mprob * (mdp - delta)).astype(BF)
            dq_out[:, full] = ((dot(ds, k) + dot(mds, mk)) * scale).astype(BF)
            dk = dot(ds, q, TN) * scale
            dv = dot(low, do, TN)
            pb[:, hf, :, at] = dk.astype(BF).reshape(WIN, tokens, width)
            pb[:, hf, :, vt] = dv.astype(BF).reshape(WIN, tokens, width)
            rg[mr, :width] = (dot(mds, q, TN) * scale).astype(BF)
            rg[mr, width:] = dot(mlow, do, TN).astype(BF)
            return 0

        lax.fori_loop(0, half, run, 0)

    def d_direct(hf):
        return rcopy(
            pb.at[p - 1, hf], rb_direct.at[hf], dd_s.at[hf], dd_r.at[hf], pos(p - 1)
        )

    def d_relay(b, hf):
        return rcopy(pb.at[b, hf], rb_relay.at[b], dr_s.at[b], dr_r.at[b], pos(5 - p))

    def d_cross(b):
        return rcopy(sumb.at[b], rb_cross.at[core], dc_s.at[b], dc_r.at[core], pos(b))

    for hf in range(2):
        head_step(hf)

        @pl.when((p >= 2) & (core != hf))
        def _():
            for b in range(2):
                d_relay(b, hf).start()

        @pl.when(core == 1)
        def _():
            d_direct(hf).start()

    per = max(slots, min(256, total_slots))

    def ship(i, _):
        first = pl.multiple_of(i * per, per)
        hot = (
            lax.broadcasted_iota(jnp.int32, (per, requests), 0) + i * per
        ) == place_row[...]
        gout[pl.ds(first, per), :] = dot(hot.astype(F32).astype(BF), rg[...]).astype(BF)
        return 0

    lax.fori_loop(0, total_slots // per, ship, 0)

    def send_grad(i, _):
        j, dev = peer_of(i)
        rcopy(rows_at(gout, j), rows_at(gin, me), grad_s, grad_r, dev).start()
        return 0

    lax.fori_loop(1, n, send_grad, 0)
    mine = pl.ds(pl.multiple_of(me * slots, slots), slots)
    gin[mine, :] = gout[mine, :]

    @pl.when(p >= 2)
    def _():
        for b in range(2):
            d_relay(b, core).wait_recv()
            sumb[b] = (pb[b, core].astype(F32) + rb_relay[b].astype(F32)).astype(BF)
            d_cross(b).start()

    for hf in range(2):
        @pl.when(core == 1)
        def _():
            dkv_out[hf] = pb[p, hf]

        @pl.when(core == 0)
        def _():
            rcopy(
                rb_direct.at[hf], rb_direct.at[hf], dd_s.at[hf], dd_r.at[hf], pos(0)
            ).wait_recv()
            dkv_out[hf] = (pb[p, hf].astype(F32) + rb_direct[hf].astype(F32)).astype(BF)

        @pl.when(p < 2)
        def _():
            rcopy(
                rb_cross.at[hf], rb_cross.at[hf], dc_s.at[hf], dc_r.at[hf], pos(0)
            ).wait_recv()
            total = pb[p, hf].astype(F32) + rb_cross[hf].astype(F32)

            @pl.when(core == 0)
            def _():
                dkv_out[hf] = (total + rb_direct[hf].astype(F32)).astype(BF)

            @pl.when(core == 1)
            def _():
                dkv_out[hf] = total.astype(BF)

    wait_bulk(gin, grad_s, grad_r).wait_recv()
    gin_out[...] = gin[...]

    rcopy(
        codes_in.at[pl.ds(0, n - 1)], codes_in.at[pl.ds(0, n - 1)], code_s, code_r, pos(0)
    ).wait_send()
    wait_bulk(rows_out, row_s, row_r).wait_send()
    wait_bulk(gout, grad_s, grad_r).wait_send()

    @pl.when(p < 2)
    def _():
        for hf in range(2):
            kv_send(hf, hf, 2 + hf).wait_send()

    @pl.when(core == 0)
    def _():
        for hf in range(2):
            kv_send(hf, 2 + hf, p + 1).wait_send()

    @pl.when(p >= 2)
    def _():
        for b in range(2):
            kv_relay(b, b).wait_send()
            d_relay(b, 1 - core).wait_send()
            d_cross(b).wait_send()

    @pl.when(core == 1)
    def _():
        for hf in range(2):
            d_direct(hf).wait_send()


def per_device(queries, keys, values, grad_out, memory, mem_index):
    _, tokens, heads, width = queries.shape
    mem_rows, mem_heads, pair = memory.shape
    index = jnp.swapaxes(mem_index[0], 0, 1)
    _, blocks_here, topk = index.shape
    requests = blocks_here * mem_heads * topk
    cycle = lax.axis_size("ctx")
    groups = lax.axis_size("dp")
    n = cycle * groups
    slots = max(2, 2 * requests // n)
    slots = (slots + 15) // 16 * 16
    lanes = (slots + 127) // 128 * 128
    total_slots = n * slots
    table_rows = mem_rows * mem_heads
    half = heads // 2

    wanted = index.reshape(requests)
    owner = wanted // mem_rows
    serial = jnp.arange(requests, dtype=jnp.int32)
    before = (owner[:, None] == owner[None, :]) & (serial[None, :] < serial[:, None])
    place = owner * slots + jnp.sum(before, axis=1, dtype=jnp.int32)
    head_of = serial // (blocks_here * topk)
    features = jnp.stack([wanted % mem_rows, head_of, jnp.ones_like(serial)]).astype(BF)
    hot = (place[:, None] == jnp.arange(total_slots, dtype=jnp.int32)[None, :]).astype(BF)
    sorted_features = dot(features, hot).astype(jnp.int32)
    codes = jnp.where(
        sorted_features[2] > 0, sorted_features[0] * mem_heads + sorted_features[1], -1
    )
    codes = jnp.pad(
        codes.reshape(n, 1, slots), ((0, 0), (0, 0), (0, lanes - slots)), constant_values=-1
    )
    q2 = queries.reshape(tokens, heads * width)
    do2 = grad_out.reshape(tokens, heads * width)
    k2 = keys.reshape(tokens, 2, half * width)
    v2 = values.reshape(tokens, 2, half * width)
    kv2 = jnp.swapaxes(jnp.concatenate([k2, v2], axis=-1), 0, 1)
    pw = 2 * half * width
    vm = pl.BlockSpec(memory_space=pltpu.VMEM)
    dma = pltpu.SemaphoreType.DMA
    dq, dkv, gin, codes_in = pl.pallas_call(
        functools.partial(
            kernel, (cycle, groups, slots, heads, width, blocks_here, topk)
        ),
        out_shape=(
            jax.ShapeDtypeStruct((tokens, heads * width), BF),
            jax.ShapeDtypeStruct((2, tokens, pw), BF),
            jax.ShapeDtypeStruct((total_slots, pair), BF),
            jax.ShapeDtypeStruct((n, 1, lanes), jnp.int32),
        ),
        in_specs=[vm] * 7,
        out_specs=(vm,) * 4,
        scratch_shapes=[
            pltpu.VMEM((n, 1, lanes), jnp.int32),
            pltpu.VMEM((total_slots, pair), BF),
            pltpu.VMEM((total_slots, pair), BF),
            pltpu.VMEM((requests, pair), BF),
            pltpu.VMEM((WIN, 2, tokens, pw), BF),
            pltpu.VMEM((WIN, 2, tokens, pw), BF),
            pltpu.VMEM((requests, pair), BF),
            pltpu.VMEM((total_slots, pair), BF),
            pltpu.VMEM((total_slots, pair), BF),
            pltpu.VMEM((2, tokens, pw), BF),
            pltpu.VMEM((2, tokens, pw), BF),
            pltpu.VMEM((2, tokens, pw), BF),
            pltpu.VMEM((2, tokens, pw), BF),
            dma, dma, dma, dma, dma, dma,
            dma((4,)), dma((WIN, 2)),
            dma((2,)), dma((2,)),
            dma((2,)), dma((2,)),
            dma((2,)), dma((2,)),
        ],
        compiler_params=pltpu.CompilerParams(
            collective_id=0, has_side_effects=True, vmem_limit_bytes=56 * 1024 * 1024
        ),
    )(codes, memory.reshape(table_rows, pair), q2, do2, kv2, place[:, None], place[None, :])
    got = codes_in[:, 0, :slots].reshape(total_slots)
    spread = (jnp.arange(table_rows, dtype=jnp.int32)[:, None] == got[None, :]).astype(BF)
    grad_table = dot(spread, gin).astype(BF)
    dkv = jnp.swapaxes(dkv, 0, 1)
    return (
        dq.reshape(1, tokens, heads, width),
        dkv[..., : half * width].reshape(1, tokens, heads, width),
        dkv[..., half * width :].reshape(1, tokens, heads, width),
        grad_table.reshape(mem_rows, mem_heads, pair),
    )


def solution(mesh):
    placed = (
        P("dp", "ctx", None, None),
        P("dp", "ctx", None, None),
        P("dp", "ctx", None, None),
        P("dp", "ctx", None, None),
        P(("ctx", "dp"), None, None),
        P("dp", "ctx", None, None),
    )
    return jax.shard_map(
        per_device,
        mesh=mesh,
        in_specs=placed,
        out_specs=(
            P("dp", "ctx", None, None),
            P("dp", "ctx", None, None),
            P("dp", "ctx", None, None),
            P(("ctx", "dp"), None, None),
        ),
        check_vma=False,
    )
```

```python
import functools

import jax
import jax.numpy as jnp
from jax import lax
from jax.experimental import pallas as pl
from jax.experimental.pallas import tpu as pltpu
from jax.sharding import PartitionSpec as P

WIN = 4
GROUPS = 4
BF = jnp.bfloat16
F32 = jnp.float32
NT = (((1,), (1,)), ((), ()))
TN = (((0,), (0,)), ((), ()))


def dot(a, b, dims=(((1,), (0,)), ((), ()))):
    return lax.dot_general(a, b, dims, preferred_element_type=F32)


def kernel(
    dims,
    codes_out, table, q_ref, do_ref, kv_ref, place_col, place_row,
    dq_out, dkv_out, table_out,
    codes_in, rows_out, returned, fetched, kvb, pb, rg, gout, gin,
    rb_direct, rb_cross, rb_relay, sumb,
    pick_mat, ship_mat, spread_mat, acc,
    code_s, code_r, row_s, row_r, grad_s, grad_r,
    kv_s, kv_r, dd_s, dd_r, dc_s, dc_r, dr_s, dr_r,
):
    cycle, groups, slots, heads, width, blocks_here, topk = dims
    n = cycle * groups
    tokens = q_ref.shape[0]
    part = heads // GROUPS
    pw = part * width
    lanes = codes_out.shape[-1]
    fold = lanes // slots
    stored = spread_mat.shape[0] > 16
    requests = place_row.shape[1]
    total_slots = n * slots
    scale = width ** (-0.5)
    c = lax.axis_index("ctx")
    d = lax.axis_index("dp")
    me = c * groups + d
    p = lax.rem(c, WIN)
    base = c - p
    core = lax.rem(p, 2)

    def peer_of(i):
        j = lax.rem(me + i, n)
        return j, {"ctx": j // groups, "dp": lax.rem(j, groups)}

    def pos(k):
        return {"ctx": base + k, "dp": d}

    def rcopy(src, dst, ss, rs, dev):
        return pltpu.make_async_remote_copy(
            src_ref=src, dst_ref=dst, send_sem=ss, recv_sem=rs,
            device_id=dev, device_id_type=pl.DeviceIdType.MESH,
        )

    barrier = pltpu.get_barrier_semaphore()

    def greet(i, _):
        _, dev = peer_of(i)
        pl.semaphore_signal(barrier, inc=1, device_id=dev, device_id_type=pl.DeviceIdType.MESH)
        return 0

    lax.fori_loop(1, n, greet, 0)
    pl.semaphore_wait(barrier, n - 1)

    def send_code(i, _):
        j, dev = peer_of(i)
        rcopy(codes_out.at[j], codes_in.at[me], code_s, code_r, dev).start()
        return 0

    lax.fori_loop(1, n, send_code, 0)

    def kv_send(g, slot, target):
        return rcopy(kv_ref.at[g], kvb.at[p, g], kv_s.at[slot], kv_r.at[p, g], pos(target))

    def kv_relay(b, k):
        g = 2 * k + core
        return rcopy(
            kvb.at[b, g], kvb.at[b, g], kv_s.at[2 * k + b], kv_r.at[b, g], pos(5 - p)
        )

    def kv_wait(b, g):
        rcopy(kvb.at[b, g], kvb.at[b, g], kv_s.at[0], kv_r.at[b, g], pos(0)).wait_recv()

    @pl.when(p < 2)
    def _():
        for g in range(GROUPS):
            kv_send(g, g, 2 + g % 2).start()

    @pl.when(core == 0)
    def _():
        for g in range(GROUPS):
            kv_send(g, GROUPS + g, p + 1).start()

    codes_in[me] = codes_out[me]
    kvb[p] = kv_ref[...]
    for s in range(1, WIN):
        @pl.when(s > p)
        def _():
            kvb[s] = jnp.zeros(kvb.shape[1:], BF)

    rcopy(
        codes_in.at[pl.ds(0, n - 1)], codes_in.at[pl.ds(0, n - 1)], code_s, code_r, pos(0)
    ).wait_recv()
    table_rows = table.shape[0]

    def rows_at(ref, j):
        return ref.at[pl.ds(pl.multiple_of(j * slots, slots), slots)]

    lane_part = lax.broadcasted_iota(jnp.int32, (1, lanes), 1) // slots

    def one_hot(hot):
        return jnp.where(hot, 1.0, 0.0).astype(BF)

    def spread_of(bundle):
        first = bundle * fold
        sel = codes_in[first]
        for k in range(1, fold):
            sel = jnp.where(lane_part == k, codes_in[first + k], sel)
        return one_hot(lax.broadcasted_iota(jnp.int32, (table_rows, lanes), 0) == sel)

    bundles = n // fold

    def serve(i, _):
        bundle = lax.rem(me // fold + i, bundles)
        at = pl.ds(pl.multiple_of(bundle * lanes, lanes), lanes)
        hot = spread_of(bundle)
        if stored:
            spread_mat[:, at] = hot
        rows_out[at, :] = dot(hot, table[...], TN).astype(BF)
        for k in range(fold):
            j = bundle * fold + k

            @pl.when(j != me)
            def _():
                rcopy(
                    rows_at(rows_out, j), rows_at(returned, me), row_s, row_r,
                    {"ctx": j // groups, "dp": lax.rem(j, groups)},
                ).start()

        return 0

    lax.fori_loop(0, bundles, serve, 0)
    mine = pl.ds(pl.multiple_of(me * slots, slots), slots)
    returned[mine, :] = rows_out[mine, :]

    chunk = min(128, requests)
    per = max(slots, min(256, total_slots))

    def chunk_at(i):
        return pl.ds(pl.multiple_of(i * chunk, chunk), chunk)

    def per_at(i):
        return pl.ds(pl.multiple_of(i * per, per), per)

    def pick_of(i):
        return one_hot(
            lax.broadcasted_iota(jnp.int32, (chunk, total_slots), 1)
            == place_col[chunk_at(i), :]
        )

    def ship_of(i):
        return one_hot(
            (lax.broadcasted_iota(jnp.int32, (per, requests), 0) + i * per) == place_row[...]
        )

    if stored:
        def fill_pick(i, _):
            pick_mat[chunk_at(i), :] = pick_of(i)
            return 0

        def fill_ship(i, _):
            ship_mat[per_at(i), :] = ship_of(i)
            return 0

        lax.fori_loop(0, requests // chunk, fill_pick, 0)
        lax.fori_loop(0, total_slots // per, fill_ship, 0)

    @pl.when(p >= 2)
    def _():
        for k in range(2):
            for b in range(2):
                kv_wait(b, 2 * k + core)
                kv_relay(b, k).start()

    @pl.when(core == 1)
    def _():
        for g in range(GROUPS):
            kv_wait(p - 1, g)

    @pl.when(p >= 2)
    def _():
        for k in range(2):
            for b in range(2):
                kv_wait(b, 2 * k + 1 - core)

    everything_else = pl.ds(0, (n - 1) * slots)

    def wait_bulk(buf, ss, rs):
        return rcopy(buf.at[everything_else], buf.at[everything_else], ss, rs, pos(0))

    wait_bulk(returned, row_s, row_r).wait_recv()

    def pick(i, _):
        hot = pick_mat[chunk_at(i), :] if stored else pick_of(i)
        fetched[chunk_at(i), :] = dot(hot, returned[...]).astype(BF)
        return 0

    lax.fori_loop(0, requests // chunk, pick, 0)

    ctx = WIN * tokens
    per_head = blocks_here * topk
    block = tokens // blocks_here
    row_id = lax.broadcasted_iota(jnp.int32, (tokens, ctx), 0)
    col_id = lax.broadcasted_iota(jnp.int32, (tokens, ctx), 1)
    live = col_id <= row_id + p * tokens
    mrow = lax.broadcasted_iota(jnp.int32, (tokens, per_head), 0)
    mcol = lax.broadcasted_iota(jnp.int32, (tokens, per_head), 1)
    mlive = (mrow // block) == (mcol // topk)

    def head_step(g):
        def run(hh, _):
            h = g * part + hh
            at = pl.ds(pl.multiple_of(hh * width, width), width)
            vt = pl.ds(pl.multiple_of(pw + hh * width, width), width)
            full = pl.ds(pl.multiple_of(h * width, width), width)
            mr = pl.ds(pl.multiple_of(h * per_head, per_head), per_head)
            q = q_ref[:, full]
            do = do_ref[:, full]
            k = kvb[:, g, :, at].reshape(ctx, width)
            v = kvb[:, g, :, vt].reshape(ctx, width)
            mk = fetched[mr, :width]
            mv = fetched[mr, width:]
            s = jnp.where(live, dot(q, k, NT) * scale, -1e30)
            ms = jnp.where(mlive, dot(q, mk, NT) * scale, -1e30)
            top = jnp.maximum(
                jnp.max(s, axis=-1, keepdims=True), jnp.max(ms, axis=-1, keepdims=True)
            )
            w = jnp.exp(s - top)
            mw = jnp.exp(ms - top)
            inv = 1.0 / (
                jnp.sum(w, axis=-1, keepdims=True) + jnp.sum(mw, axis=-1, keepdims=True)
            )
            prob = w * inv
            mprob = mw * inv
            low = prob.astype(BF)
            mlow = mprob.astype(BF)
            dp = dot(do, v, NT)
            mdp = dot(do, mv, NT)
            delta = jnp.sum(low.astype(F32) * dp, axis=-1, keepdims=True) + jnp.sum(
                mlow.astype(F32) * mdp, axis=-1, keepdims=True
            )
            ds = (prob * (dp - delta)).astype(BF)
            mds = (mprob * (mdp - delta)).astype(BF)
            dq_out[:, full] = ((dot(ds, k) + dot(mds, mk)) * scale).astype(BF)
            dk = dot(ds, q, TN) * scale
            dv = dot(low, do, TN)
            pb[:, g, :, at] = dk.astype(BF).reshape(WIN, tokens, width)
            pb[:, g, :, vt] = dv.astype(BF).reshape(WIN, tokens, width)
            rg[mr, :width] = (dot(mds, q, TN) * scale).astype(BF)
            rg[mr, width:] = dot(mlow, do, TN).astype(BF)
            return 0

        lax.fori_loop(0, part, run, 0)

    def d_direct(g):
        return rcopy(pb.at[p - 1, g], rb_direct.at[g], dd_s.at[g], dd_r.at[g], pos(p - 1))

    def d_relay(b, g, k):
        return rcopy(
            pb.at[b, g], rb_relay.at[b, k], dr_s.at[b, k], dr_r.at[b, k], pos(5 - p)
        )

    def d_cross(b, g, k):
        return rcopy(sumb.at[b, k], rb_cross.at[g], dc_s.at[b, k], dc_r.at[g], pos(b))

    def pass_on(g):
        @pl.when((p >= 2) & (core == g % 2))
        def _():
            for b in range(2):
                d_relay(b, g, g // 2).wait_recv()
                sumb[b, g // 2] = (
                    pb[b, g].astype(F32) + rb_relay[b, g // 2].astype(F32)
                ).astype(BF)
                d_cross(b, g, g // 2).start()

    for g in range(GROUPS):
        head_step(g)

        @pl.when((p >= 2) & (core != g % 2))
        def _():
            for b in range(2):
                d_relay(b, g, g // 2).start()

        @pl.when(core == 1)
        def _():
            d_direct(g).start()

        if g:
            pass_on(g - 1)

    def ship(i, _):
        hot = ship_mat[per_at(i), :] if stored else ship_of(i)
        gout[per_at(i), :] = dot(hot, rg[...]).astype(BF)
        return 0

    lax.fori_loop(0, total_slots // per, ship, 0)

    def send_grad(i, _):
        j, dev = peer_of(i)
        rcopy(rows_at(gout, j), rows_at(gin, me), grad_s, grad_r, dev).start()
        return 0

    lax.fori_loop(1, n, send_grad, 0)
    gin[mine, :] = gout[mine, :]
    pass_on(GROUPS - 1)

    def finish(g):
        @pl.when(core == 0)
        def _():
            rcopy(
                rb_direct.at[g], rb_direct.at[g], dd_s.at[g], dd_r.at[g], pos(0)
            ).wait_recv()

        @pl.when(p < 2)
        def _():
            rcopy(
                rb_cross.at[g], rb_cross.at[g], dc_s.at[0, 0], dc_r.at[g], pos(0)
            ).wait_recv()

        @pl.when(p == 0)
        def _():
            dkv_out[g] = (
                pb[0, g].astype(F32) + rb_direct[g].astype(F32) + rb_cross[g].astype(F32)
            ).astype(BF)

        @pl.when(p == 1)
        def _():
            dkv_out[g] = (pb[1, g].astype(F32) + rb_cross[g].astype(F32)).astype(BF)

        @pl.when(p == 2)
        def _():
            dkv_out[g] = (pb[2, g].astype(F32) + rb_direct[g].astype(F32)).astype(BF)

        @pl.when(p == 3)
        def _():
            dkv_out[g] = pb[3, g]

    for g in range(GROUPS):
        if g == GROUPS - 1:
            wait_bulk(gin, grad_s, grad_r).wait_recv()
            if stored:
                def spread_rows(i, _):
                    at = pl.ds(pl.multiple_of(i * 128, 128), 128)
                    table_out[at, :] = dot(spread_mat[at, :], gin[...]).astype(BF)
                    return 0

                lax.fori_loop(0, table_rows // 128, spread_rows, 0)
            else:
                acc[...] = jnp.zeros(acc.shape, F32)

                def spread_bundle(i, _):
                    at = pl.ds(pl.multiple_of(i * lanes, lanes), lanes)
                    acc[...] += dot(spread_of(i), gin[at, :])
                    return 0

                lax.fori_loop(0, bundles, spread_bundle, 0)
                table_out[...] = acc[...].astype(BF)
        finish(g)

    rcopy(
        codes_in.at[pl.ds(0, n - 1)], codes_in.at[pl.ds(0, n - 1)], code_s, code_r, pos(0)
    ).wait_send()
    wait_bulk(rows_out, row_s, row_r).wait_send()
    wait_bulk(gout, grad_s, grad_r).wait_send()

    @pl.when(p < 2)
    def _():
        for g in range(GROUPS):
            kv_send(g, g, 2 + g % 2).wait_send()

    @pl.when(core == 0)
    def _():
        for g in range(GROUPS):
            kv_send(g, GROUPS + g, p + 1).wait_send()

    @pl.when(p >= 2)
    def _():
        for k in range(2):
            for b in range(2):
                kv_relay(b, k).wait_send()
                d_relay(b, 2 * k + 1 - core, k).wait_send()
                d_cross(b, 2 * k + core, k).wait_send()

    @pl.when(core == 1)
    def _():
        for g in range(GROUPS):
            d_direct(g).wait_send()


def per_device(queries, keys, values, grad_out, memory, mem_index):
    _, tokens, heads, width = queries.shape
    mem_rows, mem_heads, pair = memory.shape
    index = jnp.swapaxes(mem_index[0], 0, 1)
    _, blocks_here, topk = index.shape
    requests = blocks_here * mem_heads * topk
    cycle = lax.axis_size("ctx")
    groups = lax.axis_size("dp")
    n = cycle * groups
    slots = max(2, 2 * requests // n)
    slots = (slots + 15) // 16 * 16
    lanes = (slots + 127) // 128 * 128
    total_slots = n * slots
    table_rows = mem_rows * mem_heads
    part = heads // GROUPS
    stored = total_slots <= 4096

    wanted = index.reshape(requests)
    owner = wanted // mem_rows
    serial = jnp.arange(requests, dtype=jnp.int32)
    before = (owner[:, None] == owner[None, :]) & (serial[None, :] < serial[:, None])
    place = owner * slots + jnp.sum(before, axis=1, dtype=jnp.int32)
    head_of = serial // (blocks_here * topk)
    features = jnp.stack([wanted % mem_rows, head_of, jnp.ones_like(serial)]).astype(BF)
    hot = (place[:, None] == jnp.arange(total_slots, dtype=jnp.int32)[None, :]).astype(BF)
    sorted_features = dot(features, hot).astype(jnp.int32)
    codes = jnp.where(
        sorted_features[2] > 0, sorted_features[0] * mem_heads + sorted_features[1], -1
    )
    codes = jnp.tile(codes.reshape(n, 1, slots), (1, 1, lanes // slots))
    q2 = queries.reshape(tokens, heads * width)
    do2 = grad_out.reshape(tokens, heads * width)
    k2 = keys.reshape(tokens, GROUPS, part * width)
    v2 = values.reshape(tokens, GROUPS, part * width)
    kv2 = jnp.swapaxes(jnp.concatenate([k2, v2], axis=-1), 0, 1)
    pw = 2 * part * width
    vm = pl.BlockSpec(memory_space=pltpu.VMEM)
    dma = pltpu.SemaphoreType.DMA
    dq, dkv, grad_table = pl.pallas_call(
        functools.partial(
            kernel, (cycle, groups, slots, heads, width, blocks_here, topk)
        ),
        out_shape=(
            jax.ShapeDtypeStruct((tokens, heads * width), BF),
            jax.ShapeDtypeStruct((GROUPS, tokens, pw), BF),
            jax.ShapeDtypeStruct((table_rows, pair), BF),
        ),
        in_specs=[vm] * 7,
        out_specs=(vm,) * 3,
        scratch_shapes=[
            pltpu.VMEM((n, 1, lanes), jnp.int32),
            pltpu.VMEM((total_slots, pair), BF),
            pltpu.VMEM((total_slots, pair), BF),
            pltpu.VMEM((requests, pair), BF),
            pltpu.VMEM((WIN, GROUPS, tokens, pw), BF),
            pltpu.VMEM((WIN, GROUPS, tokens, pw), BF),
            pltpu.VMEM((requests, pair), BF),
            pltpu.VMEM((total_slots, pair), BF),
            pltpu.VMEM((total_slots, pair), BF),
            pltpu.VMEM((GROUPS, tokens, pw), BF),
            pltpu.VMEM((GROUPS, tokens, pw), BF),
            pltpu.VMEM((2, 2, tokens, pw), BF),
            pltpu.VMEM((2, 2, tokens, pw), BF),
            pltpu.VMEM((requests, total_slots) if stored else (16, 128), BF),
            pltpu.VMEM((total_slots, requests) if stored else (16, 128), BF),
            pltpu.VMEM((table_rows, total_slots) if stored else (16, 128), BF),
            pltpu.VMEM((8, 128) if stored else (table_rows, pair), F32),
            dma, dma, dma, dma, dma, dma,
            dma((2 * GROUPS,)), dma((WIN, GROUPS)),
            dma((GROUPS,)), dma((GROUPS,)),
            dma((2, 2)), dma((GROUPS,)),
            dma((2, 2)), dma((2, 2)),
        ],
        compiler_params=pltpu.CompilerParams(
            collective_id=0, has_side_effects=True, vmem_limit_bytes=56 * 1024 * 1024
        ),
    )(codes, memory.reshape(table_rows, pair), q2, do2, kv2, place[:, None], place[None, :])
    dkv = jnp.swapaxes(dkv, 0, 1)
    return (
        dq.reshape(1, tokens, heads, width),
        dkv[..., : part * width].reshape(1, tokens, heads, width),
        dkv[..., part * width :].reshape(1, tokens, heads, width),
        grad_table.reshape(mem_rows, mem_heads, pair),
    )


def solution(mesh):
    placed = (
        P("dp", "ctx", None, None),
        P("dp", "ctx", None, None),
        P("dp", "ctx", None, None),
        P("dp", "ctx", None, None),
        P(("ctx", "dp"), None, None),
        P("dp", "ctx", None, None),
    )
    return jax.shard_map(
        per_device,
        mesh=mesh,
        in_specs=placed,
        out_specs=(
            P("dp", "ctx", None, None),
            P("dp", "ctx", None, None),
            P("dp", "ctx", None, None),
            P(("ctx", "dp"), None, None),
        ),
        check_vma=False,
    )
```

```python
import functools

import jax
import jax.numpy as jnp
from jax import lax
from jax.experimental import pallas as pl
from jax.experimental.pallas import tpu as pltpu
from jax.sharding import PartitionSpec as P

WIN = 4
GROUPS = 4
BF = jnp.bfloat16
F32 = jnp.float32
NT = (((1,), (1,)), ((), ()))
TN = (((0,), (0,)), ((), ()))


def dot(a, b, dims=(((1,), (0,)), ((), ()))):
    return lax.dot_general(a, b, dims, preferred_element_type=F32)


def kernel(
    dims,
    codes_out, table, q_ref, do_ref, kv_ref, place_col, place_row,
    dq_out, dk_out, dv_out, table_out,
    codes_in, rows_out, returned, fetched, kvb, pb, rg, gout, gin,
    rb_direct, rb_cross, rb_relay, sumb,
    pick_mat, ship_mat, spread_mat, acc,
    code_s, code_r, row_s, row_r, grad_s, grad_r,
    kv_s, kv_r, dd_s, dd_r, dc_s, dc_r, dr_s, dr_r,
):
    cycle, groups, slots, heads, width, blocks_here, topk = dims
    n = cycle * groups
    tokens = q_ref.shape[0]
    part = heads // GROUPS
    pw = part * width
    lanes = codes_out.shape[-1]
    fold = lanes // slots
    stored = spread_mat.shape[0] > 16
    requests = place_row.shape[1]
    total_slots = n * slots
    scale = width ** (-0.5)
    c = lax.axis_index("ctx")
    d = lax.axis_index("dp")
    me = c * groups + d
    p = lax.rem(c, WIN)
    base = c - p
    core = lax.rem(p, 2)

    def peer_of(i):
        j = lax.rem(me + i, n)
        return j, {"ctx": j // groups, "dp": lax.rem(j, groups)}

    def pos(k):
        return {"ctx": base + k, "dp": d}

    def rcopy(src, dst, ss, rs, dev):
        return pltpu.make_async_remote_copy(
            src_ref=src, dst_ref=dst, send_sem=ss, recv_sem=rs,
            device_id=dev, device_id_type=pl.DeviceIdType.MESH,
        )

    barrier = pltpu.get_barrier_semaphore()

    def greet(i, _):
        _, dev = peer_of(i)
        pl.semaphore_signal(barrier, inc=1, device_id=dev, device_id_type=pl.DeviceIdType.MESH)
        return 0

    lax.fori_loop(1, n, greet, 0)
    pl.semaphore_wait(barrier, n - 1)

    def send_code(i, _):
        j, dev = peer_of(i)
        rcopy(codes_out.at[j], codes_in.at[me], code_s, code_r, dev).start()
        return 0

    lax.fori_loop(1, n, send_code, 0)

    def kv_send(g, slot, target):
        return rcopy(kv_ref.at[g], kvb.at[p, g], kv_s.at[slot], kv_r.at[p, g], pos(target))

    def kv_relay(b, k):
        g = 2 * k + core
        return rcopy(
            kvb.at[b, g], kvb.at[b, g], kv_s.at[2 * k + b], kv_r.at[b, g], pos(5 - p)
        )

    def kv_wait(b, g):
        rcopy(kvb.at[b, g], kvb.at[b, g], kv_s.at[0], kv_r.at[b, g], pos(0)).wait_recv()

    def cross_sends(first):
        @pl.when(p < 2)
        def _():
            for g in (first, first + 1):
                kv_send(g, g, 2 + g % 2).start()

    cross_sends(0)

    @pl.when(core == 0)
    def _():
        for g in range(GROUPS):
            kv_send(g, GROUPS + g, p + 1).start()

    codes_in[me] = codes_out[me]
    kvb[p] = kv_ref[...]
    for s in range(1, WIN):
        @pl.when(s > p)
        def _():
            kvb[s] = jnp.zeros(kvb.shape[1:], BF)

    rcopy(
        codes_in.at[pl.ds(0, n - 1)], codes_in.at[pl.ds(0, n - 1)], code_s, code_r, pos(0)
    ).wait_recv()
    table_rows = table.shape[0]

    def rows_at(ref, j):
        return ref.at[pl.ds(pl.multiple_of(j * slots, slots), slots)]

    lane_part = lax.broadcasted_iota(jnp.int32, (1, lanes), 1) // slots

    def one_hot(hot):
        return jnp.where(hot, 1.0, 0.0).astype(BF)

    def spread_of(bundle):
        first = bundle * fold
        sel = codes_in[first]
        for k in range(1, fold):
            sel = jnp.where(lane_part == k, codes_in[first + k], sel)
        return one_hot(lax.broadcasted_iota(jnp.int32, (table_rows, lanes), 0) == sel)

    bundles = n // fold

    def serve(i, _):
        bundle = lax.rem(me // fold + i, bundles)
        at = pl.ds(pl.multiple_of(bundle * lanes, lanes), lanes)
        hot = spread_of(bundle)
        if stored:
            spread_mat[:, at] = hot
        rows_out[at, :] = dot(hot, table[...], TN).astype(BF)
        for k in range(fold):
            j = bundle * fold + k

            @pl.when(j != me)
            def _():
                rcopy(
                    rows_at(rows_out, j), rows_at(returned, me), row_s, row_r,
                    {"ctx": j // groups, "dp": lax.rem(j, groups)},
                ).start()

        return 0

    lax.fori_loop(0, bundles, serve, 0)
    cross_sends(2)
    mine = pl.ds(pl.multiple_of(me * slots, slots), slots)
    returned[mine, :] = rows_out[mine, :]

    chunk = min(128, requests)
    per = max(slots, min(256, total_slots))

    def chunk_at(i):
        return pl.ds(pl.multiple_of(i * chunk, chunk), chunk)

    def per_at(i):
        return pl.ds(pl.multiple_of(i * per, per), per)

    def pick_of(i):
        return one_hot(
            lax.broadcasted_iota(jnp.int32, (chunk, total_slots), 1)
            == place_col[chunk_at(i), :]
        )

    def ship_of(i):
        return one_hot(
            (lax.broadcasted_iota(jnp.int32, (per, requests), 0) + i * per) == place_row[...]
        )

    if stored:
        def fill_pick(i, _):
            pick_mat[chunk_at(i), :] = pick_of(i)
            return 0

        def fill_ship(i, _):
            ship_mat[per_at(i), :] = ship_of(i)
            return 0

        lax.fori_loop(0, requests // chunk, fill_pick, 0)
        lax.fori_loop(0, total_slots // per, fill_ship, 0)

    def relay_pair(k):
        @pl.when(p >= 2)
        def _():
            for b in range(2):
                kv_wait(b, 2 * k + core)
                kv_relay(b, k).start()

    def group_ready(g):
        @pl.when(core == 1)
        def _():
            kv_wait(p - 1, g)

        @pl.when((p >= 2) & (core != g % 2))
        def _():
            for b in range(2):
                kv_wait(b, g)

    relay_pair(0)

    everything_else = pl.ds(0, (n - 1) * slots)

    def wait_bulk(buf, ss, rs):
        return rcopy(buf.at[everything_else], buf.at[everything_else], ss, rs, pos(0))

    wait_bulk(returned, row_s, row_r).wait_recv()

    def pick(i, _):
        hot = pick_mat[chunk_at(i), :] if stored else pick_of(i)
        fetched[chunk_at(i), :] = dot(hot, returned[...]).astype(BF)
        return 0

    lax.fori_loop(0, requests // chunk, pick, 0)

    ctx = WIN * tokens
    per_head = blocks_here * topk
    block = tokens // blocks_here
    row_id = lax.broadcasted_iota(jnp.int32, (tokens, ctx), 0)
    col_id = lax.broadcasted_iota(jnp.int32, (tokens, ctx), 1)
    live = col_id <= row_id + p * tokens
    mrow = lax.broadcasted_iota(jnp.int32, (tokens, per_head), 0)
    mcol = lax.broadcasted_iota(jnp.int32, (tokens, per_head), 1)
    mlive = (mrow // block) == (mcol // topk)

    def head_step(g):
        def run(hh, _):
            h = g * part + hh
            at = pl.ds(pl.multiple_of(hh * width, width), width)
            vt = pl.ds(pl.multiple_of(pw + hh * width, width), width)
            full = pl.ds(pl.multiple_of(h * width, width), width)
            mr = pl.ds(pl.multiple_of(h * per_head, per_head), per_head)
            q = q_ref[:, full]
            do = do_ref[:, full]
            k = kvb[:, g, :, at].reshape(ctx, width)
            v = kvb[:, g, :, vt].reshape(ctx, width)
            mk = fetched[mr, :width]
            mv = fetched[mr, width:]
            s = jnp.where(live, dot(q, k, NT) * scale, -1e30)
            ms = jnp.where(mlive, dot(q, mk, NT) * scale, -1e30)
            top = jnp.maximum(
                jnp.max(s, axis=-1, keepdims=True), jnp.max(ms, axis=-1, keepdims=True)
            )
            w = jnp.exp(s - top)
            mw = jnp.exp(ms - top)
            inv = 1.0 / (
                jnp.sum(w, axis=-1, keepdims=True) + jnp.sum(mw, axis=-1, keepdims=True)
            )
            prob = w * inv
            mprob = mw * inv
            low = prob.astype(BF)
            mlow = mprob.astype(BF)
            dp = dot(do, v, NT)
            mdp = dot(do, mv, NT)
            delta = jnp.sum(low.astype(F32) * dp, axis=-1, keepdims=True) + jnp.sum(
                mlow.astype(F32) * mdp, axis=-1, keepdims=True
            )
            ds = (prob * (dp - delta)).astype(BF)
            mds = (mprob * (mdp - delta)).astype(BF)
            dq_out[:, full] = ((dot(ds, k) + dot(mds, mk)) * scale).astype(BF)
            dk = dot(ds, q, TN) * scale
            dv = dot(low, do, TN)
            pb[:, g, :, at] = dk.astype(BF).reshape(WIN, tokens, width)
            pb[:, g, :, vt] = dv.astype(BF).reshape(WIN, tokens, width)
            rg[mr, :width] = (dot(mds, q, TN) * scale).astype(BF)
            rg[mr, width:] = dot(mlow, do, TN).astype(BF)
            return 0

        lax.fori_loop(0, part, run, 0)

    def d_direct(g):
        return rcopy(pb.at[p - 1, g], rb_direct.at[g], dd_s.at[g], dd_r.at[g], pos(p - 1))

    def d_relay(b, g, k):
        return rcopy(
            pb.at[b, g], rb_relay.at[b, k], dr_s.at[b, k], dr_r.at[b, k], pos(5 - p)
        )

    def d_cross(b, g, k):
        return rcopy(sumb.at[b, k], rb_cross.at[g], dc_s.at[b, k], dc_r.at[g], pos(b))

    def pass_on(g):
        @pl.when((p >= 2) & (core == g % 2))
        def _():
            for b in range(2):
                d_relay(b, g, g // 2).wait_recv()
                sumb[b, g // 2] = (
                    pb[b, g].astype(F32) + rb_relay[b, g // 2].astype(F32)
                ).astype(BF)
                d_cross(b, g, g // 2).start()

    for g in range(GROUPS):
        if g == 1:
            relay_pair(1)
        group_ready(g)
        head_step(g)

        @pl.when((p >= 2) & (core != g % 2))
        def _():
            for b in range(2):
                d_relay(b, g, g // 2).start()

        @pl.when(core == 1)
        def _():
            d_direct(g).start()

        if g:
            pass_on(g - 1)

    def ship(i, _):
        hot = ship_mat[per_at(i), :] if stored else ship_of(i)
        gout[per_at(i), :] = dot(hot, rg[...]).astype(BF)
        return 0

    lax.fori_loop(0, total_slots // per, ship, 0)

    def send_grad(i, _):
        j, dev = peer_of(i)
        rcopy(rows_at(gout, j), rows_at(gin, me), grad_s, grad_r, dev).start()
        return 0

    lax.fori_loop(1, n, send_grad, 0)
    gin[mine, :] = gout[mine, :]
    pass_on(GROUPS - 1)

    def finish(g):
        @pl.when(core == 0)
        def _():
            rcopy(
                rb_direct.at[g], rb_direct.at[g], dd_s.at[g], dd_r.at[g], pos(0)
            ).wait_recv()

        @pl.when(p < 2)
        def _():
            rcopy(
                rb_cross.at[g], rb_cross.at[g], dc_s.at[0, 0], dc_r.at[g], pos(0)
            ).wait_recv()

        cols = pl.ds(g * pw, pw)

        def put(total):
            dk_out[:, cols] = total[:, :pw].astype(BF)
            dv_out[:, cols] = total[:, pw:].astype(BF)

        @pl.when(p == 0)
        def _():
            put(pb[0, g].astype(F32) + rb_direct[g].astype(F32) + rb_cross[g].astype(F32))

        @pl.when(p == 1)
        def _():
            put(pb[1, g].astype(F32) + rb_cross[g].astype(F32))

        @pl.when(p == 2)
        def _():
            put(pb[2, g].astype(F32) + rb_direct[g].astype(F32))

        @pl.when(p == 3)
        def _():
            put(pb[3, g])

    for g in range(GROUPS):
        if g == GROUPS - 1:
            wait_bulk(gin, grad_s, grad_r).wait_recv()
            if stored:
                def spread_rows(i, _):
                    at = pl.ds(pl.multiple_of(i * 128, 128), 128)
                    table_out[at, :] = dot(spread_mat[at, :], gin[...]).astype(BF)
                    return 0

                lax.fori_loop(0, table_rows // 128, spread_rows, 0)
            else:
                acc[...] = jnp.zeros(acc.shape, F32)

                def spread_bundle(i, _):
                    at = pl.ds(pl.multiple_of(i * lanes, lanes), lanes)
                    acc[...] += dot(spread_of(i), gin[at, :])
                    return 0

                lax.fori_loop(0, bundles, spread_bundle, 0)
                table_out[...] = acc[...].astype(BF)
        finish(g)

    rcopy(
        codes_in.at[pl.ds(0, n - 1)], codes_in.at[pl.ds(0, n - 1)], code_s, code_r, pos(0)
    ).wait_send()
    wait_bulk(rows_out, row_s, row_r).wait_send()
    wait_bulk(gout, grad_s, grad_r).wait_send()

    @pl.when(p < 2)
    def _():
        for g in range(GROUPS):
            kv_send(g, g, 2 + g % 2).wait_send()

    @pl.when(core == 0)
    def _():
        for g in range(GROUPS):
            kv_send(g, GROUPS + g, p + 1).wait_send()

    @pl.when(p >= 2)
    def _():
        for k in range(2):
            for b in range(2):
                kv_relay(b, k).wait_send()
                d_relay(b, 2 * k + 1 - core, k).wait_send()
                d_cross(b, 2 * k + core, k).wait_send()

    @pl.when(core == 1)
    def _():
        for g in range(GROUPS):
            d_direct(g).wait_send()


def per_device(queries, keys, values, grad_out, memory, mem_index):
    _, tokens, heads, width = queries.shape
    mem_rows, mem_heads, pair = memory.shape
    index = jnp.swapaxes(mem_index[0], 0, 1)
    _, blocks_here, topk = index.shape
    requests = blocks_here * mem_heads * topk
    cycle = lax.axis_size("ctx")
    groups = lax.axis_size("dp")
    n = cycle * groups
    slots = max(2, 2 * requests // n)
    slots = (slots + 15) // 16 * 16
    lanes = (slots + 127) // 128 * 128
    total_slots = n * slots
    table_rows = mem_rows * mem_heads
    part = heads // GROUPS
    stored = total_slots <= 4096

    wanted = index.reshape(requests)
    owner = wanted // mem_rows
    serial = jnp.arange(requests, dtype=jnp.int32)
    before = (owner[:, None] == owner[None, :]) & (serial[None, :] < serial[:, None])
    place = owner * slots + jnp.sum(before, axis=1, dtype=jnp.int32)
    head_of = serial // (blocks_here * topk)
    features = jnp.stack([wanted % mem_rows, head_of, jnp.ones_like(serial)]).astype(BF)
    hot = (place[:, None] == jnp.arange(total_slots, dtype=jnp.int32)[None, :]).astype(BF)
    sorted_features = dot(features, hot).astype(jnp.int32)
    codes = jnp.where(
        sorted_features[2] > 0, sorted_features[0] * mem_heads + sorted_features[1], -1
    )
    codes = jnp.tile(codes.reshape(n, 1, slots), (1, 1, lanes // slots))
    q2 = queries.reshape(tokens, heads * width)
    do2 = grad_out.reshape(tokens, heads * width)
    k2 = keys.reshape(tokens, GROUPS, part * width)
    v2 = values.reshape(tokens, GROUPS, part * width)
    kv2 = jnp.swapaxes(jnp.concatenate([k2, v2], axis=-1), 0, 1)
    pw = 2 * part * width
    vm = pl.BlockSpec(memory_space=pltpu.VMEM)
    dma = pltpu.SemaphoreType.DMA
    dq, dk, dv, grad_table = pl.pallas_call(
        functools.partial(
            kernel, (cycle, groups, slots, heads, width, blocks_here, topk)
        ),
        out_shape=(
            jax.ShapeDtypeStruct((tokens, heads * width), BF),
            jax.ShapeDtypeStruct((tokens, heads * width), BF),
            jax.ShapeDtypeStruct((tokens, heads * width), BF),
            jax.ShapeDtypeStruct((table_rows, pair), BF),
        ),
        in_specs=[vm] * 7,
        out_specs=(vm,) * 4,
        scratch_shapes=[
            pltpu.VMEM((n, 1, lanes), jnp.int32),
            pltpu.VMEM((total_slots, pair), BF),
            pltpu.VMEM((total_slots, pair), BF),
            pltpu.VMEM((requests, pair), BF),
            pltpu.VMEM((WIN, GROUPS, tokens, pw), BF),
            pltpu.VMEM((WIN, GROUPS, tokens, pw), BF),
            pltpu.VMEM((requests, pair), BF),
            pltpu.VMEM((total_slots, pair), BF),
            pltpu.VMEM((total_slots, pair), BF),
            pltpu.VMEM((GROUPS, tokens, pw), BF),
            pltpu.VMEM((GROUPS, tokens, pw), BF),
            pltpu.VMEM((2, 2, tokens, pw), BF),
            pltpu.VMEM((2, 2, tokens, pw), BF),
            pltpu.VMEM((requests, total_slots) if stored else (16, 128), BF),
            pltpu.VMEM((total_slots, requests) if stored else (16, 128), BF),
            pltpu.VMEM((table_rows, total_slots) if stored else (16, 128), BF),
            pltpu.VMEM((8, 128) if stored else (table_rows, pair), F32),
            dma, dma, dma, dma, dma, dma,
            dma((2 * GROUPS,)), dma((WIN, GROUPS)),
            dma((GROUPS,)), dma((GROUPS,)),
            dma((2, 2)), dma((GROUPS,)),
            dma((2, 2)), dma((2, 2)),
        ],
        compiler_params=pltpu.CompilerParams(
            collective_id=0, has_side_effects=True, vmem_limit_bytes=56 * 1024 * 1024
        ),
    )(codes, memory.reshape(table_rows, pair), q2, do2, kv2, place[:, None], place[None, :])
    return (
        dq.reshape(1, tokens, heads, width),
        dk.reshape(1, tokens, heads, width),
        dv.reshape(1, tokens, heads, width),
        grad_table.reshape(mem_rows, mem_heads, pair),
    )


def solution(mesh):
    placed = (
        P("dp", "ctx", None, None),
        P("dp", "ctx", None, None),
        P("dp", "ctx", None, None),
        P("dp", "ctx", None, None),
        P(("ctx", "dp"), None, None),
        P("dp", "ctx", None, None),
    )
    return jax.shard_map(
        per_device,
        mesh=mesh,
        in_specs=placed,
        out_specs=(
            P("dp", "ctx", None, None),
            P("dp", "ctx", None, None),
            P("dp", "ctx", None, None),
            P(("ctx", "dp"), None, None),
        ),
        check_vma=False,
    )
```

```python
import functools

import jax
import jax.numpy as jnp
from jax import lax
from jax.experimental import pallas as pl
from jax.experimental.pallas import tpu as pltpu
from jax.sharding import PartitionSpec as P

WIN = 4
GROUPS = 4
BF = jnp.bfloat16
F32 = jnp.float32
NT = (((1,), (1,)), ((), ()))
TN = (((0,), (0,)), ((), ()))


def dot(a, b, dims=(((1,), (0,)), ((), ()))):
    return lax.dot_general(a, b, dims, preferred_element_type=F32)


def kernel(
    dims,
    codes_out, table, q_ref, do_ref, kv_ref, place_col, place_row,
    dq_out, dk_out, dv_out, table_out,
    codes_in, rows_out, returned, fetched, kvb, pb, rg, gout, gin,
    rb_direct, rb_cross, rb_relay, sumb,
    pick_mat, ship_mat, spread_mat, acc,
    code_s, code_r, row_s, row_r, grad_s, grad_r,
    kv_s, kv_r, dd_s, dd_r, dc_s, dc_r, dr_s, dr_r,
):
    cycle, groups, slots, heads, width, blocks_here, topk = dims
    n = cycle * groups
    tokens = q_ref.shape[0]
    part = heads // GROUPS
    pw = part * width
    lanes = codes_out.shape[-1]
    fold = lanes // slots
    stored = spread_mat.shape[0] > 16
    requests = place_row.shape[1]
    total_slots = n * slots
    scale = width ** (-0.5)
    c = lax.axis_index("ctx")
    d = lax.axis_index("dp")
    me = c * groups + d
    p = lax.rem(c, WIN)
    base = c - p
    core = lax.rem(p, 2)

    def peer_of(i):
        j = lax.rem(me + i, n)
        return j, {"ctx": j // groups, "dp": lax.rem(j, groups)}

    def pos(k):
        return {"ctx": base + k, "dp": d}

    def rcopy(src, dst, ss, rs, dev):
        return pltpu.make_async_remote_copy(
            src_ref=src, dst_ref=dst, send_sem=ss, recv_sem=rs,
            device_id=dev, device_id_type=pl.DeviceIdType.MESH,
        )

    barrier = pltpu.get_barrier_semaphore()

    def greet(i, _):
        _, dev = peer_of(i)
        pl.semaphore_signal(barrier, inc=1, device_id=dev, device_id_type=pl.DeviceIdType.MESH)
        return 0

    lax.fori_loop(1, n, greet, 0)
    pl.semaphore_wait(barrier, n - 1)

    def send_code(i, _):
        j, dev = peer_of(i)
        rcopy(codes_out.at[j], codes_in.at[me], code_s, code_r, dev).start()
        return 0

    lax.fori_loop(1, n, send_code, 0)

    def kv_send(g, slot, target):
        return rcopy(kv_ref.at[g], kvb.at[p, g], kv_s.at[slot], kv_r.at[p, g], pos(target))

    def kv_relay(b, k):
        g = 2 * k + core
        return rcopy(
            kvb.at[b, g], kvb.at[b, g], kv_s.at[2 * k + b], kv_r.at[b, g], pos(5 - p)
        )

    def kv_wait(b, g):
        rcopy(kvb.at[b, g], kvb.at[b, g], kv_s.at[0], kv_r.at[b, g], pos(0)).wait_recv()

    def cross_sends(first):
        @pl.when(p < 2)
        def _():
            for g in (first, first + 1):
                kv_send(g, g, 2 + g % 2).start()

    cross_sends(0)

    @pl.when(core == 0)
    def _():
        for g in range(GROUPS):
            kv_send(g, GROUPS + g, p + 1).start()

    codes_in[me] = codes_out[me]
    kvb[p] = kv_ref[...]
    for s in range(1, WIN):
        @pl.when(s > p)
        def _():
            kvb[s] = jnp.zeros(kvb.shape[1:], BF)

    rcopy(
        codes_in.at[pl.ds(0, n - 1)], codes_in.at[pl.ds(0, n - 1)], code_s, code_r, pos(0)
    ).wait_recv()
    table_rows = table.shape[0]

    def rows_at(ref, j):
        return ref.at[pl.ds(pl.multiple_of(j * slots, slots), slots)]

    lane_part = lax.broadcasted_iota(jnp.int32, (1, lanes), 1) // slots

    def one_hot(hot):
        return jnp.where(hot, 1.0, 0.0).astype(BF)

    def spread_of(bundle):
        first = bundle * fold
        sel = codes_in[first]
        for k in range(1, fold):
            sel = jnp.where(lane_part == k, codes_in[first + k], sel)
        return one_hot(lax.broadcasted_iota(jnp.int32, (table_rows, lanes), 0) == sel)

    bundles = n // fold

    def serve(i, _):
        bundle = lax.rem(me // fold + i, bundles)
        at = pl.ds(pl.multiple_of(bundle * lanes, lanes), lanes)
        hot = spread_of(bundle)
        if stored:
            spread_mat[:, at] = hot
        rows_out[at, :] = dot(hot, table[...], TN).astype(BF)
        for k in range(fold):
            j = bundle * fold + k

            @pl.when(j != me)
            def _():
                rcopy(
                    rows_at(rows_out, j), rows_at(returned, me), row_s, row_r,
                    {"ctx": j // groups, "dp": lax.rem(j, groups)},
                ).start()

        return 0

    lax.fori_loop(0, bundles, serve, 0)
    cross_sends(2)
    mine = pl.ds(pl.multiple_of(me * slots, slots), slots)
    returned[mine, :] = rows_out[mine, :]

    chunk = min(128, requests)
    per = max(slots, min(256, total_slots))

    def chunk_at(i):
        return pl.ds(pl.multiple_of(i * chunk, chunk), chunk)

    def per_at(i):
        return pl.ds(pl.multiple_of(i * per, per), per)

    def pick_of(i):
        return one_hot(
            lax.broadcasted_iota(jnp.int32, (chunk, total_slots), 1)
            == place_col[chunk_at(i), :]
        )

    def ship_of(i):
        return one_hot(
            (lax.broadcasted_iota(jnp.int32, (per, requests), 0) + i * per) == place_row[...]
        )

    if stored:
        def fill_pick(i, _):
            pick_mat[chunk_at(i), :] = pick_of(i)
            return 0

        def fill_ship(i, _):
            ship_mat[per_at(i), :] = ship_of(i)
            return 0

        lax.fori_loop(0, requests // chunk, fill_pick, 0)
        lax.fori_loop(0, total_slots // per, fill_ship, 0)

    def relay_pair(k):
        @pl.when(p >= 2)
        def _():
            for b in range(2):
                kv_wait(b, 2 * k + core)
                kv_relay(b, k).start()

    def group_ready(g):
        @pl.when(core == 1)
        def _():
            kv_wait(p - 1, g)

        @pl.when((p >= 2) & (core != g % 2))
        def _():
            for b in range(2):
                kv_wait(b, g)

    relay_pair(0)

    everything_else = pl.ds(0, (n - 1) * slots)

    def wait_bulk(buf, ss, rs):
        return rcopy(buf.at[everything_else], buf.at[everything_else], ss, rs, pos(0))

    wait_bulk(returned, row_s, row_r).wait_recv()

    def pick(i, _):
        hot = pick_mat[chunk_at(i), :] if stored else pick_of(i)
        fetched[chunk_at(i), :] = dot(hot, returned[...]).astype(BF)
        return 0

    lax.fori_loop(0, requests // chunk, pick, 0)

    ctx = WIN * tokens
    per_head = blocks_here * topk
    block = tokens // blocks_here
    row_id = lax.broadcasted_iota(jnp.int32, (tokens, ctx), 0)
    col_id = lax.broadcasted_iota(jnp.int32, (tokens, ctx), 1)
    live = col_id <= row_id + p * tokens
    mrow = lax.broadcasted_iota(jnp.int32, (tokens, per_head), 0)
    mcol = lax.broadcasted_iota(jnp.int32, (tokens, per_head), 1)
    mlive = (mrow // block) == (mcol // topk)

    def head_step(g):
        def run(hh, _):
            h = g * part + hh
            at = pl.ds(pl.multiple_of(hh * width, width), width)
            vt = pl.ds(pl.multiple_of(pw + hh * width, width), width)
            full = pl.ds(pl.multiple_of(h * width, width), width)
            mr = pl.ds(pl.multiple_of(h * per_head, per_head), per_head)
            q = q_ref[:, full]
            do = do_ref[:, full]
            k = kvb[:, g, :, at].reshape(ctx, width)
            v = kvb[:, g, :, vt].reshape(ctx, width)
            mk = fetched[mr, :width]
            mv = fetched[mr, width:]
            s = jnp.where(live, dot(q, k, NT) * scale, -1e30)
            ms = jnp.where(mlive, dot(q, mk, NT) * scale, -1e30)
            top = jnp.maximum(
                jnp.max(s, axis=-1, keepdims=True), jnp.max(ms, axis=-1, keepdims=True)
            )
            w = jnp.exp(s - top)
            mw = jnp.exp(ms - top)
            inv = 1.0 / (
                jnp.sum(w, axis=-1, keepdims=True) + jnp.sum(mw, axis=-1, keepdims=True)
            )
            prob = w * inv
            mprob = mw * inv
            low = prob.astype(BF)
            mlow = mprob.astype(BF)
            dp = dot(do, v, NT)
            mdp = dot(do, mv, NT)
            delta = jnp.sum(low.astype(F32) * dp, axis=-1, keepdims=True) + jnp.sum(
                mlow.astype(F32) * mdp, axis=-1, keepdims=True
            )
            ds = (prob * (dp - delta)).astype(BF)
            mds = (mprob * (mdp - delta)).astype(BF)
            dq_out[:, full] = ((dot(ds, k) + dot(mds, mk)) * scale).astype(BF)
            dk = dot(ds, q, TN) * scale
            dv = dot(low, do, TN)
            pb[:, g, :, at] = dk.astype(BF).reshape(WIN, tokens, width)
            pb[:, g, :, vt] = dv.astype(BF).reshape(WIN, tokens, width)
            rg[mr, :width] = (dot(mds, q, TN) * scale).astype(BF)
            rg[mr, width:] = dot(mlow, do, TN).astype(BF)
            return 0

        lax.fori_loop(0, part, run, 0, unroll=True)

    def d_direct(g):
        return rcopy(pb.at[p - 1, g], rb_direct.at[g], dd_s.at[g], dd_r.at[g], pos(p - 1))

    def d_relay(b, g, k):
        return rcopy(
            pb.at[b, g], rb_relay.at[b, k], dr_s.at[b, k], dr_r.at[b, k], pos(5 - p)
        )

    def d_cross(b, g, k):
        return rcopy(sumb.at[b, k], rb_cross.at[g], dc_s.at[b, k], dc_r.at[g], pos(b))

    def pass_on(g):
        @pl.when((p >= 2) & (core == g % 2))
        def _():
            for b in range(2):
                d_relay(b, g, g // 2).wait_recv()
                sumb[b, g // 2] = (
                    pb[b, g].astype(F32) + rb_relay[b, g // 2].astype(F32)
                ).astype(BF)
                d_cross(b, g, g // 2).start()

    for g in range(GROUPS):
        if g == 1:
            relay_pair(1)
        group_ready(g)
        head_step(g)

        @pl.when((p >= 2) & (core != g % 2))
        def _():
            for b in range(2):
                d_relay(b, g, g // 2).start()

        @pl.when(core == 1)
        def _():
            d_direct(g).start()

        if g:
            pass_on(g - 1)

    def ship(i, _):
        hot = ship_mat[per_at(i), :] if stored else ship_of(i)
        gout[per_at(i), :] = dot(hot, rg[...]).astype(BF)
        return 0

    lax.fori_loop(0, total_slots // per, ship, 0)

    def send_grad(i, _):
        j, dev = peer_of(i)
        rcopy(rows_at(gout, j), rows_at(gin, me), grad_s, grad_r, dev).start()
        return 0

    lax.fori_loop(1, n, send_grad, 0)
    gin[mine, :] = gout[mine, :]
    pass_on(GROUPS - 1)

    def finish(g):
        @pl.when(core == 0)
        def _():
            rcopy(
                rb_direct.at[g], rb_direct.at[g], dd_s.at[g], dd_r.at[g], pos(0)
            ).wait_recv()

        @pl.when(p < 2)
        def _():
            rcopy(
                rb_cross.at[g], rb_cross.at[g], dc_s.at[0, 0], dc_r.at[g], pos(0)
            ).wait_recv()

        cols = pl.ds(g * pw, pw)

        def put(total):
            dk_out[:, cols] = total[:, :pw].astype(BF)
            dv_out[:, cols] = total[:, pw:].astype(BF)

        @pl.when(p == 0)
        def _():
            put(pb[0, g].astype(F32) + rb_direct[g].astype(F32) + rb_cross[g].astype(F32))

        @pl.when(p == 1)
        def _():
            put(pb[1, g].astype(F32) + rb_cross[g].astype(F32))

        @pl.when(p == 2)
        def _():
            put(pb[2, g].astype(F32) + rb_direct[g].astype(F32))

        @pl.when(p == 3)
        def _():
            put(pb[3, g])

    for g in range(GROUPS):
        if g == GROUPS - 1:
            wait_bulk(gin, grad_s, grad_r).wait_recv()
            if stored:
                def spread_rows(i, _):
                    at = pl.ds(pl.multiple_of(i * 128, 128), 128)
                    table_out[at, :] = dot(spread_mat[at, :], gin[...]).astype(BF)
                    return 0

                lax.fori_loop(0, table_rows // 128, spread_rows, 0)
            else:
                acc[...] = jnp.zeros(acc.shape, F32)

                def spread_bundle(i, _):
                    at = pl.ds(pl.multiple_of(i * lanes, lanes), lanes)
                    acc[...] += dot(spread_of(i), gin[at, :])
                    return 0

                lax.fori_loop(0, bundles, spread_bundle, 0)
                table_out[...] = acc[...].astype(BF)
        finish(g)

    rcopy(
        codes_in.at[pl.ds(0, n - 1)], codes_in.at[pl.ds(0, n - 1)], code_s, code_r, pos(0)
    ).wait_send()
    wait_bulk(rows_out, row_s, row_r).wait_send()
    wait_bulk(gout, grad_s, grad_r).wait_send()

    @pl.when(p < 2)
    def _():
        for g in range(GROUPS):
            kv_send(g, g, 2 + g % 2).wait_send()

    @pl.when(core == 0)
    def _():
        for g in range(GROUPS):
            kv_send(g, GROUPS + g, p + 1).wait_send()

    @pl.when(p >= 2)
    def _():
        for k in range(2):
            for b in range(2):
                kv_relay(b, k).wait_send()
                d_relay(b, 2 * k + 1 - core, k).wait_send()
                d_cross(b, 2 * k + core, k).wait_send()

    @pl.when(core == 1)
    def _():
        for g in range(GROUPS):
            d_direct(g).wait_send()


def per_device(queries, keys, values, grad_out, memory, mem_index):
    _, tokens, heads, width = queries.shape
    mem_rows, mem_heads, pair = memory.shape
    index = jnp.swapaxes(mem_index[0], 0, 1)
    _, blocks_here, topk = index.shape
    requests = blocks_here * mem_heads * topk
    cycle = lax.axis_size("ctx")
    groups = lax.axis_size("dp")
    n = cycle * groups
    slots = max(2, 2 * requests // n)
    slots = (slots + 15) // 16 * 16
    lanes = (slots + 127) // 128 * 128
    total_slots = n * slots
    table_rows = mem_rows * mem_heads
    part = heads // GROUPS
    stored = total_slots <= 4096

    wanted = index.reshape(requests)
    owner = wanted // mem_rows
    serial = jnp.arange(requests, dtype=jnp.int32)
    before = (owner[:, None] == owner[None, :]) & (serial[None, :] < serial[:, None])
    place = owner * slots + jnp.sum(before, axis=1, dtype=jnp.int32)
    head_of = serial // (blocks_here * topk)
    features = jnp.stack([wanted % mem_rows, head_of, jnp.ones_like(serial)]).astype(BF)
    hot = (place[:, None] == jnp.arange(total_slots, dtype=jnp.int32)[None, :]).astype(BF)
    sorted_features = dot(features, hot).astype(jnp.int32)
    codes = jnp.where(
        sorted_features[2] > 0, sorted_features[0] * mem_heads + sorted_features[1], -1
    )
    codes = jnp.tile(codes.reshape(n, 1, slots), (1, 1, lanes // slots))
    q2 = queries.reshape(tokens, heads * width)
    do2 = grad_out.reshape(tokens, heads * width)
    k2 = keys.reshape(tokens, GROUPS, part * width)
    v2 = values.reshape(tokens, GROUPS, part * width)
    kv2 = jnp.swapaxes(jnp.concatenate([k2, v2], axis=-1), 0, 1)
    pw = 2 * part * width
    vm = pl.BlockSpec(memory_space=pltpu.VMEM)
    dma = pltpu.SemaphoreType.DMA
    dq, dk, dv, grad_table = pl.pallas_call(
        functools.partial(
            kernel, (cycle, groups, slots, heads, width, blocks_here, topk)
        ),
        out_shape=(
            jax.ShapeDtypeStruct((tokens, heads * width), BF),
            jax.ShapeDtypeStruct((tokens, heads * width), BF),
            jax.ShapeDtypeStruct((tokens, heads * width), BF),
            jax.ShapeDtypeStruct((table_rows, pair), BF),
        ),
        in_specs=[vm] * 7,
        out_specs=(vm,) * 4,
        scratch_shapes=[
            pltpu.VMEM((n, 1, lanes), jnp.int32),
            pltpu.VMEM((total_slots, pair), BF),
            pltpu.VMEM((total_slots, pair), BF),
            pltpu.VMEM((requests, pair), BF),
            pltpu.VMEM((WIN, GROUPS, tokens, pw), BF),
            pltpu.VMEM((WIN, GROUPS, tokens, pw), BF),
            pltpu.VMEM((requests, pair), BF),
            pltpu.VMEM((total_slots, pair), BF),
            pltpu.VMEM((total_slots, pair), BF),
            pltpu.VMEM((GROUPS, tokens, pw), BF),
            pltpu.VMEM((GROUPS, tokens, pw), BF),
            pltpu.VMEM((2, 2, tokens, pw), BF),
            pltpu.VMEM((2, 2, tokens, pw), BF),
            pltpu.VMEM((requests, total_slots) if stored else (16, 128), BF),
            pltpu.VMEM((total_slots, requests) if stored else (16, 128), BF),
            pltpu.VMEM((table_rows, total_slots) if stored else (16, 128), BF),
            pltpu.VMEM((8, 128) if stored else (table_rows, pair), F32),
            dma, dma, dma, dma, dma, dma,
            dma((2 * GROUPS,)), dma((WIN, GROUPS)),
            dma((GROUPS,)), dma((GROUPS,)),
            dma((2, 2)), dma((GROUPS,)),
            dma((2, 2)), dma((2, 2)),
        ],
        compiler_params=pltpu.CompilerParams(
            collective_id=0, has_side_effects=True, vmem_limit_bytes=56 * 1024 * 1024
        ),
    )(codes, memory.reshape(table_rows, pair), q2, do2, kv2, place[:, None], place[None, :])
    return (
        dq.reshape(1, tokens, heads, width),
        dk.reshape(1, tokens, heads, width),
        dv.reshape(1, tokens, heads, width),
        grad_table.reshape(mem_rows, mem_heads, pair),
    )


def solution(mesh):
    placed = (
        P("dp", "ctx", None, None),
        P("dp", "ctx", None, None),
        P("dp", "ctx", None, None),
        P("dp", "ctx", None, None),
        P(("ctx", "dp"), None, None),
        P("dp", "ctx", None, None),
    )
    return jax.shard_map(
        per_device,
        mesh=mesh,
        in_specs=placed,
        out_specs=(
            P("dp", "ctx", None, None),
            P("dp", "ctx", None, None),
            P("dp", "ctx", None, None),
            P(("ctx", "dp"), None, None),
        ),
        check_vma=False,
    )
```
